32 devices in a mesh: dp: 8 (over z, x), tensor: 4 (over y, core).
Axes of the slice: x: 2, y: 2, z: 4, core: 2. Of those that a mesh axis runs over, the one named last changes fastest.
Arguments:
- images: bfloat16 [8, 257, 1024], P('dp'), may hold values from -6 to 6
- upstream: bfloat16 [8, 257, 1024], P('dp'), may hold values from -6 to 6
- placed: int32 [8], P('dp'), may hold values from 0 to 1, as said below
- attn_gain: bfloat16 [2, 1024], replicated, may hold values from 0.25 to 1.75
- attn_shift: bfloat16 [2, 1024], replicated, may hold values from -4 to 4
- qkv_weight: bfloat16 [2, 1024, 3, 1024], P(None, None, None, 'tensor'), may hold values from -0.1875 to 0.1875
- qv_bias: bfloat16 [2, 2, 1024], P(None, None, 'tensor'), may hold values from -6 to 6
- proj_weight: bfloat16 [2, 1024, 1024], P(None, 'tensor'), may hold values from -0.75 to 0.75
- proj_bias: bfloat16 [2, 1024], replicated, may hold values from -6 to 6
- mlp_gain: bfloat16 [2, 1024], replicated, may hold values from 0.25 to 1.75
- mlp_shift: bfloat16 [2, 1024], replicated, may hold values from -4 to 4
- up_weight: bfloat16 [2, 1024, 4096], P(None, None, 'tensor'), may hold values from -0.1875 to 0.1875
- up_bias: bfloat16 [2, 4096], P(None, 'tensor'), may hold values from -6 to 6
- down_weight: bfloat16 [2, 4096, 1024], P(None, 'tensor'), may hold values from -0.09375 to 0.09375
- down_bias: bfloat16 [2, 1024], replicated, may hold values from -6 to 6
Outputs:
- outputs: bfloat16 [8, 257, 1024], P('dp')
- images_grad: bfloat16 [8, 257, 1024], P('dp')
- attn_gain_grad: float32 [2, 1024], P(None, 'dp')
- attn_shift_grad: float32 [2, 1024], P(None, 'dp')
- qkv_weight_grad: float32 [2, 1024, 3, 1024], P(None, 'dp', None, 'tensor')
- qv_bias_grad: float32 [2, 2, 1024], P(None, None, ('tensor', 'dp'))
- proj_weight_grad: float32 [2, 1024, 1024], P(None, 'tensor', 'dp')
- proj_bias_grad: float32 [2, 1024], P(None, 'dp')
- mlp_gain_grad: float32 [2, 1024], P(None, 'dp')
- mlp_shift_grad: float32 [2, 1024], P(None, 'dp')
- up_weight_grad: float32 [2, 1024, 4096], P(None, 'dp', 'tensor')
- up_bias_grad: float32 [2, 4096], P(None, ('tensor', 'dp'))
- down_weight_grad: float32 [2, 4096, 1024], P(None, 'tensor', 'dp')
- down_bias_grad: float32 [2, 1024], P(None, 'dp')
The draws below stay inside these ranges and needn't reach their ends.
Inputs may be any that keep to these rules, and one draw needn't show every extreme that they name: `placed`: 1 where the slot holds an image and 0 where it is empty; the first slot always holds one and at least one slot is empty.
All inputs are finite; a program needn't handle non-finite values.
Results may differ from the reference program's by a relative error of at most 0.02.
Values may be sent and summed in bfloat16 or wider, within the bound.
A program may use at most 192 MiB of HBM per device.

```python
import jax
import jax.numpy as jnp
from jax import lax

D = 1024
HEAD_DIM = 64
FF = 4096
SEQ = 257
LAYERS = 2
IMAGES = 8
N_TENSOR = 4


def draw_placed(key, part):
    key = jax.random.fold_in(key, 11)
    pick_key, hole_key = jax.random.split(key)
    selected_positions = jax.random.randint(pick_key, (IMAGES,), 0, 4)
    occupancy_flags = (selected_positions > 0).astype(jnp.int32)
    vacant_position = jax.random.randint(hole_key, (), 1, IMAGES)
    occupancy_flags = occupancy_flags.at[vacant_position].set(0)
    return occupancy_flags.at[0].set(1)


def with_spikes(entries, stream_key, source, target, parts, factor):
    def block_of(axis_at):
        return (jnp.arange(entries.shape[axis_at]) // (entries.shape[axis_at] // parts)).reshape((-1,) + (1,) * (entries.ndim - 1 - axis_at))

    near = jax.random.permutation(stream_key, parts)[block_of(target)]
    second = (block_of(target) + parts // 2) % parts
    return jnp.where((block_of(source) == near) | (block_of(source) == second), factor * entries, entries)


def block_levels(own_key, shape, cuts, least, high):
    loudness = 1.0
    for axis_at, blocks in cuts:
        heights = jax.random.uniform(jax.random.fold_in(jax.random.fold_in(own_key, 6), axis_at), (blocks,), jnp.float32, least / len(cuts), high / len(cuts))
        loudness = loudness * jnp.repeat(jnp.exp(heights), shape[axis_at] // blocks).reshape((-1,) + (1,) * (len(shape) - 1 - axis_at))
    return loudness


def scatter_about(stream_key, shape, spread, limit, cuts=(), held_as=jnp.bfloat16):
    values = jax.random.normal(stream_key, shape, jnp.float32) * spread
    if len(cuts) > 0:
        values = block_levels(stream_key, shape, cuts, -0.22, 0.18) * values
    return jnp.clip(values, min=-limit, max=limit).astype(held_as)


def noise_with(stream_key, shape, spread, limit, cuts, heavy, held_as=jnp.bfloat16):
    drawn = spread * jax.random.normal(stream_key, shape, jnp.float32)
    if cuts:
        drawn = drawn * block_levels(stream_key, shape, cuts, -0.22, 0.18)
    return jnp.clip(with_spikes(drawn, jax.random.fold_in(stream_key, 3), *heavy), -limit, limit).astype(held_as)


def setup_inputs(seed: int = 0) -> dict:
    keys = jax.random.split(jax.random.key(seed), 16)
    images = scatter_about(keys[0], (IMAGES, SEQ, D), 1.0, 6.0, ((0, 8),))
    upstream = noise_with(keys[1], (IMAGES, SEQ, D), 1.0, 6.0, ((0, 8),), (0, 2, 8, 2.0))
    placed = draw_placed(jax.random.fold_in(keys[15], 71), 0)
    attn_gain = jnp.clip(1.0 + 0.15 * jax.random.normal(keys[3], (LAYERS, D), jnp.float32), 0.25, 1.75).astype(jnp.bfloat16)
    attn_shift = scatter_about(keys[4], (LAYERS, D), 0.3, 4.0)
    qkv_weight = scatter_about(keys[5], (LAYERS, D, 3, D), D ** -0.5, 0.1875, ((3, 4),))
    qv_bias = scatter_about(keys[6], (LAYERS, 2, D), 0.5, 6.0, ((2, 4),))
    proj_weight = scatter_about(keys[7], (LAYERS, D, D), (D // 16) ** -0.5, 0.75, ((1, 4),))
    proj_bias = scatter_about(keys[8], (LAYERS, D), 0.5, 6.0)
    mlp_gain = jnp.clip(1.0 + 0.15 * jax.random.normal(keys[9], (LAYERS, D), jnp.float32), 0.25, 1.75).astype(jnp.bfloat16)
    mlp_shift = scatter_about(keys[10], (LAYERS, D), 0.3, 4.0)
    up_weight = scatter_about(keys[11], (LAYERS, D, FF), D ** -0.5, 0.1875, ((2, 4),))
    up_bias = scatter_about(keys[12], (LAYERS, FF), 0.5, 6.0, ((1, 4),))
    down_weight = scatter_about(keys[13], (LAYERS, FF, D), FF ** -0.5, 0.09375, ((1, 4),))
    down_bias = scatter_about(keys[14], (LAYERS, D), 0.5, 6.0)
    return {"images": images, "upstream": upstream, "placed": placed, "attn_gain": attn_gain, "attn_shift": attn_shift, "qkv_weight": qkv_weight, "qv_bias": qv_bias, "proj_weight": proj_weight, "proj_bias": proj_bias, "mlp_gain": mlp_gain, "mlp_shift": mlp_shift, "up_weight": up_weight, "up_bias": up_bias, "down_weight": down_weight, "down_bias": down_bias}


EPS = 1e-06
HIGH = lax.Precision.HIGHEST

@jax.custom_vjp
def low(v):
    return lax.optimization_barrier(v.astype(jnp.bfloat16)).astype(jnp.float32)

@jax.custom_vjp
def low_back(v):
    return v

def low_keep(v):
    return (low(v), None)

def low_pass(kept, grad):
    return (grad,)

def back_keep(v):
    return (v, None)

def back_low(kept, grad):
    return (low(grad),)
low.defvjp(low_keep, low_pass)
low_back.defvjp(back_keep, back_low)

def layer_norm(vector, scale_gain, offset):
    average = lax.optimization_barrier(jnp.mean(vector, axis=-1, keepdims=True))
    centered = vector - average
    variance = lax.optimization_barrier(jnp.mean(centered * centered, axis=-1, keepdims=True))
    return centered * lax.rsqrt(variance + EPS) * scale_gain + offset

def product(first_op, second_op):
    return jnp.dot(first_op, second_op, precision=HIGH)

def attention(queries, key_rows, value_rows):
    scores = jnp.einsum('qhe,khe->hqk', queries, key_rows, precision=HIGH) * HEAD_DIM ** (-0.5)
    chances = jax.nn.softmax(low_back(scores), axis=-1)
    return jnp.einsum('hqk,khe->qhe', low(chances), value_rows, precision=HIGH)

def layer(hidden, weights):
    attn_gain, attn_shift, qkv_weight, qv_bias, proj_weight, proj_bias, mlp_gain, mlp_shift, up_weight, up_bias, down_weight, down_bias = weights
    local_width = D // N_TENSOR
    head_count = local_width // HEAD_DIM
    head_shape = (SEQ, head_count, HEAD_DIM)
    normed = low(layer_norm(hidden, attn_gain, attn_shift))
    attn_total = jnp.zeros_like(hidden)
    for member in range(N_TENSOR):
        columns = slice(member * local_width, (member + 1) * local_width)
        source = low_back(normed)
        queries = low(low_back(product(source, qkv_weight[:, 0, columns]) + qv_bias[0, columns]))
        key_rows = low(low_back(product(source, qkv_weight[:, 1, columns])))
        value_rows = low(low_back(product(source, qkv_weight[:, 2, columns]) + qv_bias[1, columns]))
        context = attention(queries.reshape(head_shape), key_rows.reshape(head_shape), value_rows.reshape(head_shape))
        context = low(low_back(context.reshape(SEQ, local_width)))
        attn_total = attn_total + low(product(context, proj_weight[columns, :]))
    residual = hidden + low_back(attn_total) + proj_bias
    mlp_input = low(layer_norm(residual, mlp_gain, mlp_shift))
    hidden_width = FF // N_TENSOR
    mlp_total = jnp.zeros_like(hidden)
    for member in range(N_TENSOR):
        columns = slice(member * hidden_width, (member + 1) * hidden_width)
        pre_act = low_back(product(low_back(mlp_input), up_weight[:, columns]) + up_bias[columns])
        activ = low(jax.nn.gelu(pre_act, approximate=False))
        mlp_total = mlp_total + low(product(activ, down_weight[columns, :]))
    return residual + low_back(mlp_total) + down_bias

def forward(picture_sample, params):
    for layer_index in range(LAYERS):
        picture_sample = layer(picture_sample, tuple((param[layer_index] for param in params)))
    return picture_sample

def reference(images, upstream, placed, attn_gain, attn_shift, qkv_weight, qv_bias, proj_weight, proj_bias, mlp_gain, mlp_shift, up_weight, up_bias, down_weight, down_bias):
    params = tuple((param.astype(jnp.float32) for param in (attn_gain, attn_shift, qkv_weight, qv_bias, proj_weight, proj_bias, mlp_gain, mlp_shift, up_weight, up_bias, down_weight, down_bias)))

    def accumulate(totals, entry_item):
        picture_sample, incoming_adjoint, occupancy_flags = entry_item
        retain_mask = occupancy_flags.astype(jnp.float32)
        result, pullback = jax.vjp(forward, picture_sample.astype(jnp.float32), params)
        image_grad, param_grads = pullback(incoming_adjoint.astype(jnp.float32) * retain_mask)
        totals = jax.tree.map(jnp.add, totals, param_grads)
        return (totals, ((result * retain_mask).astype(jnp.bfloat16), image_grad.astype(jnp.bfloat16)))
    initial = jax.tree.map(jnp.zeros_like, params)
    totals, (outputs, images_grad) = lax.scan(accumulate, initial, (images, upstream, placed))
    return (outputs, images_grad, totals[0], totals[1], totals[2], totals[3], totals[4], totals[5], totals[6], totals[7], totals[8], totals[9], totals[10], totals[11])
```

```python
import functools

import jax
import jax.numpy as jnp
from jax import lax
from jax.experimental import pallas as pl
from jax.experimental.pallas import tpu as pltpu
from jax.sharding import PartitionSpec as P

HEAD_DIM = 64
SEQ = 257
LAYERS = 2


EPS = 1e-06
EXTRA_ROWS = 16
CHUNKS = 2


def product_sum_kernel(
    transposed,
    left_ref,
    weight_ref,
    out_ref,
    send_pair,
    got_pair,
    send_far,
    got_far,
    send_done,
    got_done,
    send_sems,
    recv_sems,
):
    me = lax.axis_index("tensor")
    side = lax.rem(me, 2)
    pair = me + 1 - 2 * side
    far = lax.rem(me + 2, 4)
    rows = left_ref.shape[0]
    half = out_ref.shape[1] // 2
    part = half // CHUNKS

    barrier = pltpu.get_barrier_semaphore()
    for other in (pair, far):
        pl.semaphore_signal(
            barrier, inc=1, device_id={"tensor": other}, device_id_type=pl.DeviceIdType.MESH
        )

    def product(owner, chunk):
        span = pl.ds(pl.multiple_of(owner * half + chunk * part, part), part)
        if transposed:
            return lax.dot_general(
                left_ref[...],
                weight_ref[0, span, :],
                (((1,), (1,)), ((), ())),
                preferred_element_type=jnp.float32,
            )
        return jnp.dot(left_ref[...], weight_ref[0, :, span], preferred_element_type=jnp.float32)

    def copy_of(stage, chunk, source, target, other):
        return pltpu.make_async_remote_copy(
            src_ref=source.at[chunk],
            dst_ref=target.at[chunk],
            send_sem=send_sems.at[stage, chunk],
            recv_sem=recv_sems.at[stage, chunk],
            device_id={"tensor": other},
            device_id_type=pl.DeviceIdType.MESH,
        )

    to_pair = [copy_of(0, chunk, send_pair, got_pair, pair) for chunk in range(CHUNKS)]
    to_far = [copy_of(1, chunk, send_far, got_far, far) for chunk in range(CHUNKS)]
    to_done = [copy_of(2, chunk, send_done, got_done, pair) for chunk in range(CHUNKS)]

    for chunk in range(CHUNKS):
        send_pair[chunk, :rows, :] = product(1 - side, chunk).astype(jnp.bfloat16)
        if chunk == 0:
            pl.semaphore_wait(barrier, 2)
        to_pair[chunk].start()
    for chunk in range(CHUNKS):
        mine = product(side, chunk).astype(jnp.bfloat16).astype(jnp.float32)
        to_pair[chunk].wait_recv()
        send_far[chunk, :rows, :] = (
            mine + got_pair[chunk, :rows, :].astype(jnp.float32)
        ).astype(jnp.bfloat16)
        to_far[chunk].start()
    for chunk in range(CHUNKS):
        to_far[chunk].wait_recv()
        total = (
            send_far[chunk, :rows, :].astype(jnp.float32)
            + got_far[chunk, :rows, :].astype(jnp.float32)
        ).astype(jnp.bfloat16)
        send_done[chunk, :rows, :] = total
        to_done[chunk].start()
        out_ref[:, pl.ds(pl.multiple_of(side * half + chunk * part, part), part)] = total
    for chunk in range(CHUNKS):
        to_done[chunk].wait_recv()
        out_ref[:, pl.ds(pl.multiple_of((1 - side) * half + chunk * part, part), part)] = got_done[
            chunk, :rows, :
        ]
    for chunk in range(CHUNKS):
        to_pair[chunk].wait_send()
        to_far[chunk].wait_send()
        to_done[chunk].wait_send()


def product_sum(left, weight, layer_index, transposed, call_id):
    rows, depth = left.shape
    columns = weight.shape[1] if transposed else weight.shape[2]
    held_rows = -(-rows // 16) * 16
    buffer = pltpu.VMEM((CHUNKS, held_rows, columns // 2 // CHUNKS), jnp.bfloat16)
    return pl.pallas_call(
        functools.partial(product_sum_kernel, transposed),
        grid=(1,),
        out_shape=jax.ShapeDtypeStruct((rows, columns), jnp.bfloat16),
        in_specs=[
            pl.BlockSpec((rows, depth), lambda step: (0, 0)),
            pl.BlockSpec((1,) + weight.shape[1:], lambda step: (layer_index, 0, 0)),
        ],
        out_specs=pl.BlockSpec((rows, columns), lambda step: (0, 0)),
        scratch_shapes=[buffer] * 6
        + [pltpu.SemaphoreType.DMA((3, CHUNKS)), pltpu.SemaphoreType.DMA((3, CHUNKS))],
        compiler_params=pltpu.CompilerParams(
            collective_id=call_id, has_side_effects=True, vmem_limit_bytes=24 * 2**20
        ),
        cost_estimate=pl.CostEstimate(
            flops=2 * rows * depth * columns,
            bytes_accessed=2 * (rows * depth + depth * columns + rows * columns),
            transcendentals=0,
        ),
    )(left, weight)


def layer_norm(vector, scale_gain, offset):
    average = jnp.mean(vector, axis=-1, keepdims=True)
    centered = vector - average
    variance = jnp.mean(centered * centered, axis=-1, keepdims=True)
    return centered * lax.rsqrt(variance + EPS) * scale_gain + offset


def gelu_exact(vector):
    return jax.nn.gelu(vector, approximate=False)


def row_sum(matrix):
    return jnp.sum(matrix.astype(jnp.float32), axis=0)


def split_heads(matrix, slot_count):
    return matrix.reshape(slot_count, SEQ, matrix.shape[1] // HEAD_DIM, HEAD_DIM)


def scores_of(queries, key_rows):
    raw_scores = jnp.einsum(
        "sqhe,skhe->shqk", queries, key_rows, preferred_element_type=jnp.float32
    )
    return raw_scores * HEAD_DIM ** (-0.5)


def attend(queries, key_rows, value_rows):
    scores = scores_of(queries, key_rows)
    row_max = jnp.max(scores, axis=-1, keepdims=True)
    row_total = jnp.sum(jnp.exp(scores - row_max), axis=-1, keepdims=True)
    log_norm = row_max + jnp.log(row_total)
    chances = jnp.exp(scores - log_norm).astype(jnp.bfloat16)
    context = jnp.einsum("shqk,skhe->sqhe", chances, value_rows, preferred_element_type=jnp.float32)
    return (context, log_norm)


def attend_back(queries, key_rows, value_rows, log_norm, context_grad):
    chances = jnp.exp(scores_of(queries, key_rows) - log_norm)
    chance_grad = jnp.einsum(
        "sqhe,skhe->shqk", context_grad, value_rows, preferred_element_type=jnp.float32
    )
    value_grad = jnp.einsum(
        "shqk,sqhe->skhe",
        chances.astype(jnp.bfloat16),
        context_grad,
        preferred_element_type=jnp.float32,
    )
    inner = jnp.sum(chance_grad * chances, axis=-1, keepdims=True)
    score_grad = (chances * (chance_grad - inner)).astype(jnp.bfloat16)
    query_grad = jnp.einsum(
        "shqk,skhe->sqhe", score_grad, key_rows, preferred_element_type=jnp.float32
    ) * HEAD_DIM ** (-0.5)
    key_grad = jnp.einsum(
        "shqk,sqhe->skhe", score_grad, queries, preferred_element_type=jnp.float32
    ) * HEAD_DIM ** (-0.5)
    return (query_grad, key_grad, value_grad)


def layer_forward(hidden, weights, whole, layer_index, slot_count):
    (
        attn_gain,
        attn_shift,
        qkv_weight,
        qv_bias,
        proj_weight,
        proj_bias,
        mlp_gain,
        mlp_shift,
        up_weight,
        up_bias,
        down_weight,
        down_bias,
    ) = weights
    local_width = qkv_weight.shape[2]
    qkv_flat = whole[0][layer_index]
    normed = layer_norm(hidden, attn_gain, attn_shift).astype(jnp.bfloat16)
    joined = jnp.dot(normed, qkv_flat, preferred_element_type=jnp.float32).reshape(
        -1, 3, local_width
    )
    queries = (joined[:, 0] + qv_bias[0]).astype(jnp.bfloat16)
    key_rows = joined[:, 1].astype(jnp.bfloat16)
    value_rows = (joined[:, 2] + qv_bias[1]).astype(jnp.bfloat16)
    context, log_norm = attend(
        split_heads(queries, slot_count),
        split_heads(key_rows, slot_count),
        split_heads(value_rows, slot_count),
    )
    context = context.reshape(-1, local_width).astype(jnp.bfloat16)
    attn_total = product_sum(context, whole[1], layer_index, False, 4 * layer_index)
    residual = hidden + attn_total.astype(jnp.float32) + proj_bias
    mlp_input = layer_norm(residual, mlp_gain, mlp_shift).astype(jnp.bfloat16)
    pre_act = jnp.dot(mlp_input, up_weight, preferred_element_type=jnp.float32) + up_bias
    activ = gelu_exact(pre_act).astype(jnp.bfloat16)
    mlp_total = product_sum(activ, whole[3], layer_index, False, 4 * layer_index + 1)
    output = residual + mlp_total.astype(jnp.float32) + down_bias
    saved = (
        hidden,
        normed,
        queries,
        key_rows,
        value_rows,
        log_norm,
        context,
        residual,
        mlp_input,
        pre_act,
        activ,
    )
    return (output, saved)


def layer_backward(out_grad, weights, whole, layer_index, saved, slot_count):
    (
        attn_gain,
        attn_shift,
        qkv_weight,
        qv_bias,
        proj_weight,
        proj_bias,
        mlp_gain,
        mlp_shift,
        up_weight,
        up_bias,
        down_weight,
        down_bias,
    ) = weights
    (
        hidden,
        normed,
        queries,
        key_rows,
        value_rows,
        log_norm,
        context,
        residual,
        mlp_input,
        pre_act,
        activ,
    ) = saved
    local_width = qkv_weight.shape[2]
    down_bias_grad = row_sum(out_grad)
    branch_grad = out_grad.astype(jnp.bfloat16)
    down_weight_grad = jnp.einsum(
        "rd,rf->df", branch_grad, activ, preferred_element_type=jnp.float32
    )
    activ_grad = jnp.einsum(
        "rd,fd->rf", branch_grad, down_weight, preferred_element_type=jnp.float32
    )
    gelu_pull = jax.vjp(gelu_exact, pre_act)[1]
    pre_grad = gelu_pull(activ_grad)[0].astype(jnp.bfloat16)
    up_bias_grad = row_sum(pre_grad)
    up_weight_grad = jnp.einsum(
        "rd,rf->df", mlp_input, pre_grad, preferred_element_type=jnp.float32
    )
    mlp_input_grad = product_sum(pre_grad, whole[2], layer_index, True, 4 * layer_index + 2)
    mlp_input_grad = mlp_input_grad.astype(jnp.float32)
    mlp_pull = jax.vjp(
        layer_norm, residual, mlp_gain.astype(jnp.float32), mlp_shift.astype(jnp.float32)
    )[1]
    resid_part, mlp_gain_grad, mlp_shift_grad = mlp_pull(mlp_input_grad)
    residual_grad = out_grad + resid_part
    proj_bias_grad = row_sum(residual_grad)
    attn_branch = residual_grad.astype(jnp.bfloat16)
    proj_weight_grad = jnp.einsum(
        "rd,rc->dc", attn_branch, context, preferred_element_type=jnp.float32
    )
    context_grad = jnp.einsum(
        "rd,cd->rc", attn_branch, proj_weight, preferred_element_type=jnp.float32
    ).astype(jnp.bfloat16)
    query_grad, key_grad, value_grad = attend_back(
        split_heads(queries, slot_count),
        split_heads(key_rows, slot_count),
        split_heads(value_rows, slot_count),
        log_norm,
        split_heads(context_grad, slot_count),
    )
    query_grad = query_grad.reshape(-1, local_width).astype(jnp.bfloat16)
    key_grad = key_grad.reshape(-1, local_width).astype(jnp.bfloat16)
    value_grad = value_grad.reshape(-1, local_width).astype(jnp.bfloat16)
    qv_bias_grad = jnp.stack([row_sum(query_grad), row_sum(value_grad)])
    flat_grad = jnp.stack([query_grad, key_grad, value_grad], axis=1).reshape(-1, 3 * local_width)
    qkv_weight_grad = jnp.einsum(
        "rd,rc->dc", normed, flat_grad, preferred_element_type=jnp.float32
    )
    normed_grad = product_sum(flat_grad, whole[0], layer_index, True, 4 * layer_index + 3)
    normed_grad = normed_grad.astype(jnp.float32)
    attn_pull = jax.vjp(
        layer_norm, hidden, attn_gain.astype(jnp.float32), attn_shift.astype(jnp.float32)
    )[1]
    hidden_part, attn_gain_grad, attn_shift_grad = attn_pull(normed_grad)
    grads = (
        attn_gain_grad,
        attn_shift_grad,
        qkv_weight_grad,
        qv_bias_grad,
        proj_weight_grad,
        proj_bias_grad,
        mlp_gain_grad,
        mlp_shift_grad,
        up_weight_grad,
        up_bias_grad,
        down_weight_grad,
        down_bias_grad,
    )
    return (residual_grad + hidden_part, grads)


def pack_grads(grads, members):
    (
        attn_gain_grad,
        attn_shift_grad,
        qkv_weight_grad,
        qv_bias_grad,
        proj_weight_grad,
        proj_bias_grad,
        mlp_gain_grad,
        mlp_shift_grad,
        up_weight_grad,
        up_bias_grad,
        down_weight_grad,
        down_bias_grad,
    ) = [grad.astype(jnp.bfloat16) for grad in grads]
    wide = jnp.concatenate(
        [up_weight_grad, down_weight_grad, qkv_weight_grad, proj_weight_grad], axis=1
    )
    width = wide.shape[1]
    wide = wide.reshape(members, -1, width)
    small = [
        vector.reshape(members, -1)
        for vector in (
            attn_gain_grad,
            attn_shift_grad,
            proj_bias_grad,
            mlp_gain_grad,
            mlp_shift_grad,
            down_bias_grad,
            up_bias_grad,
            qv_bias_grad[0],
            qv_bias_grad[1],
        )
    ]
    small = jnp.concatenate(small, axis=1)
    small = jnp.pad(small, ((0, 0), (0, width - small.shape[1])))
    small = jnp.pad(small[:, None, :], ((0, 0), (0, EXTRA_ROWS - 1), (0, 0)))
    return jnp.concatenate([wide, small], axis=1)


def sum_layer(grads):
    members = lax.axis_size("dp")
    local_hidden = grads[8].shape[1]
    local_width = grads[4].shape[1]
    model_width = grads[0].shape[0]
    packed = pack_grads(grads, members)
    packed = packed.reshape(-1, packed.shape[2])
    summed = lax.psum_scatter(packed, "dp", scatter_dimension=0, tiled=True)
    summed = summed.astype(jnp.float32)
    rows = summed[:-EXTRA_ROWS]
    cuts = [0]
    for part in (local_hidden, local_hidden, 3 * local_width, local_width):
        cuts.append(cuts[-1] + part)
    up_part, down_part, qkv_part, proj_part = [
        rows[:, cuts[i] : cuts[i + 1]] for i in range(4)
    ]
    line = summed[-EXTRA_ROWS]
    sizes = [model_width // members] * 6 + [local_hidden // members] + [local_width // members] * 2
    vectors = []
    at = 0
    for size in sizes:
        vectors.append(line[at : at + size])
        at += size
    return (
        vectors[0],
        vectors[1],
        qkv_part.reshape(-1, 3, local_width),
        jnp.stack([vectors[7], vectors[8]]),
        proj_part.T,
        vectors[2],
        vectors[3],
        vectors[4],
        up_part,
        vectors[6],
        down_part.T,
        vectors[5],
    )


def on_device(
    images,
    upstream,
    placed,
    attn_gain,
    attn_shift,
    qkv_weight,
    qv_bias,
    proj_weight,
    proj_bias,
    mlp_gain,
    mlp_shift,
    up_weight,
    up_bias,
    down_weight,
    down_bias,
):
    slot_count = images.shape[0]
    row_count = slot_count * images.shape[1]
    model_width = images.shape[2]
    retain_mask = placed.astype(jnp.float32)[:, None, None]
    params = (
        attn_gain,
        attn_shift,
        qkv_weight,
        qv_bias,
        proj_weight,
        proj_bias,
        mlp_gain,
        mlp_shift,
        up_weight,
        up_bias,
        down_weight,
        down_bias,
    )
    qkv_whole = qkv_weight.reshape(qkv_weight.shape[0], qkv_weight.shape[1], -1)
    whole = (qkv_whole, proj_weight, up_weight, down_weight)
    hidden = images.reshape(row_count, model_width).astype(jnp.float32)
    saved_layers = []
    for layer_index in range(LAYERS):
        weights = tuple((param[layer_index] for param in params))
        hidden, saved = layer_forward(hidden, weights, whole, layer_index, slot_count)
        saved_layers.append(saved)
    outputs = (hidden.reshape(images.shape) * retain_mask).astype(jnp.bfloat16)
    carried = (upstream.astype(jnp.float32) * retain_mask).reshape(row_count, model_width)
    collected = [None] * LAYERS
    for layer_index in reversed(range(LAYERS)):
        weights = tuple((param[layer_index] for param in params))
        carried, layer_grads = layer_backward(
            carried, weights, whole, layer_index, saved_layers[layer_index], slot_count
        )
        collected[layer_index] = sum_layer(layer_grads)
    stacked = tuple(
        (
            jnp.stack([collected[layer_index][member] for layer_index in range(LAYERS)])
            for member in range(12)
        )
    )
    images_grad = carried.reshape(images.shape).astype(jnp.bfloat16)
    return (
        outputs,
        images_grad,
        stacked[0],
        stacked[1],
        stacked[2],
        stacked[3],
        stacked[4],
        stacked[5],
        stacked[6],
        stacked[7],
        stacked[8],
        stacked[9],
        stacked[10],
        stacked[11],
    )


def solution(mesh):
    return jax.shard_map(
        on_device,
        mesh=mesh,
        in_specs=(
            P("dp", None, None),
            P("dp", None, None),
            P("dp"),
            P(),
            P(),
            P(None, None, None, "tensor"),
            P(None, None, "tensor"),
            P(None, "tensor", None),
            P(),
            P(),
            P(),
            P(None, None, "tensor"),
            P(None, "tensor"),
            P(None, "tensor", None),
            P(),
        ),
        out_specs=(
            P("dp", None, None),
            P("dp", None, None),
            P(None, "dp"),
            P(None, "dp"),
            P(None, "dp", None, "tensor"),
            P(None, None, ("tensor", "dp")),
            P(None, "tensor", "dp"),
            P(None, "dp"),
            P(None, "dp"),
            P(None, "dp"),
            P(None, "dp", "tensor"),
            P(None, ("tensor", "dp")),
            P(None, "tensor", "dp"),
            P(None, "dp"),
        ),
        check_vma=False,
    )
```

```python
import functools

import jax
import jax.numpy as jnp
from jax import lax
from jax.experimental import pallas as pl
from jax.experimental.pallas import tpu as pltpu
from jax.sharding import PartitionSpec as P

HEAD_DIM = 64
SEQ = 257
LAYERS = 2


EPS = 1e-06
CHUNKS = 2


def product_sum_kernel(
    transposed,
    left_ref,
    weight_ref,
    out_ref,
    send_pair,
    got_pair,
    send_far,
    got_far,
    send_done,
    got_done,
    send_sems,
    recv_sems,
):
    me = lax.axis_index("tensor")
    side = lax.rem(me, 2)
    pair = me + 1 - 2 * side
    far = lax.rem(me + 2, 4)
    rows = left_ref.shape[0]
    half = out_ref.shape[1] // 2
    part = half // CHUNKS

    barrier = pltpu.get_barrier_semaphore()
    for other in (pair, far):
        pl.semaphore_signal(
            barrier, inc=1, device_id={"tensor": other}, device_id_type=pl.DeviceIdType.MESH
        )

    def product(owner, chunk):
        span = pl.ds(pl.multiple_of(owner * half + chunk * part, part), part)
        if transposed:
            return lax.dot_general(
                left_ref[...],
                weight_ref[0, span, :],
                (((1,), (1,)), ((), ())),
                preferred_element_type=jnp.float32,
            )
        return jnp.dot(left_ref[...], weight_ref[0, :, span], preferred_element_type=jnp.float32)

    def copy_of(stage, chunk, source, target, other):
        return pltpu.make_async_remote_copy(
            src_ref=source.at[chunk],
            dst_ref=target.at[chunk],
            send_sem=send_sems.at[stage, chunk],
            recv_sem=recv_sems.at[stage, chunk],
            device_id={"tensor": other},
            device_id_type=pl.DeviceIdType.MESH,
        )

    to_pair = [copy_of(0, chunk, send_pair, got_pair, pair) for chunk in range(CHUNKS)]
    to_far = [copy_of(1, chunk, send_far, got_far, far) for chunk in range(CHUNKS)]
    to_done = [copy_of(2, chunk, send_done, got_done, pair) for chunk in range(CHUNKS)]

    for chunk in range(CHUNKS):
        send_pair[chunk, :rows, :] = product(1 - side, chunk).astype(jnp.bfloat16)
        if chunk == 0:
            pl.semaphore_wait(barrier, 2)
        to_pair[chunk].start()
    for chunk in range(CHUNKS):
        mine = product(side, chunk).astype(jnp.bfloat16).astype(jnp.float32)
        to_pair[chunk].wait_recv()
        send_far[chunk, :rows, :] = (
            mine + got_pair[chunk, :rows, :].astype(jnp.float32)
        ).astype(jnp.bfloat16)
        to_far[chunk].start()
    for chunk in range(CHUNKS):
        to_far[chunk].wait_recv()
        total = (
            send_far[chunk, :rows, :].astype(jnp.float32)
            + got_far[chunk, :rows, :].astype(jnp.float32)
        ).astype(jnp.bfloat16)
        send_done[chunk, :rows, :] = total
        to_done[chunk].start()
        out_ref[:, pl.ds(pl.multiple_of(side * half + chunk * part, part), part)] = total
    for chunk in range(CHUNKS):
        to_done[chunk].wait_recv()
        out_ref[:, pl.ds(pl.multiple_of((1 - side) * half + chunk * part, part), part)] = got_done[
            chunk, :rows, :
        ]
    for chunk in range(CHUNKS):
        to_pair[chunk].wait_send()
        to_far[chunk].wait_send()
        to_done[chunk].wait_send()


def product_sum(left, weight, layer_index, transposed, call_id):
    rows, depth = left.shape
    columns = weight.shape[1] if transposed else weight.shape[2]
    held_rows = -(-rows // 16) * 16
    buffer = pltpu.VMEM((CHUNKS, held_rows, columns // 2 // CHUNKS), jnp.bfloat16)
    return pl.pallas_call(
        functools.partial(product_sum_kernel, transposed),
        grid=(1,),
        out_shape=jax.ShapeDtypeStruct((rows, columns), jnp.bfloat16),
        in_specs=[
            pl.BlockSpec((rows, depth), lambda step: (0, 0)),
            pl.BlockSpec((1,) + weight.shape[1:], lambda step: (layer_index, 0, 0)),
        ],
        out_specs=pl.BlockSpec((rows, columns), lambda step: (0, 0)),
        scratch_shapes=[buffer] * 6
        + [pltpu.SemaphoreType.DMA((3, CHUNKS)), pltpu.SemaphoreType.DMA((3, CHUNKS))],
        compiler_params=pltpu.CompilerParams(
            collective_id=call_id, has_side_effects=True, vmem_limit_bytes=24 * 2**20
        ),
        cost_estimate=pl.CostEstimate(
            flops=2 * rows * depth * columns,
            bytes_accessed=2 * (rows * depth + depth * columns + rows * columns),
            transcendentals=0,
        ),
    )(left, weight)


def layer_norm(vector, scale_gain, offset):
    average = jnp.mean(vector, axis=-1, keepdims=True)
    centered = vector - average
    variance = jnp.mean(centered * centered, axis=-1, keepdims=True)
    return centered * lax.rsqrt(variance + EPS) * scale_gain + offset


def gelu_exact(vector):
    return jax.nn.gelu(vector, approximate=False)


def row_sum(matrix):
    return jnp.sum(matrix.astype(jnp.float32), axis=0)


def split_heads(matrix, slot_count):
    return matrix.reshape(slot_count, SEQ, matrix.shape[1] // HEAD_DIM, HEAD_DIM)


def scores_of(queries, key_rows):
    raw_scores = jnp.einsum(
        "sqhe,skhe->shqk", queries, key_rows, preferred_element_type=jnp.float32
    )
    return raw_scores * HEAD_DIM ** (-0.5)


def attend(queries, key_rows, value_rows):
    scores = scores_of(queries, key_rows)
    row_max = jnp.max(scores, axis=-1, keepdims=True)
    row_total = jnp.sum(jnp.exp(scores - row_max), axis=-1, keepdims=True)
    log_norm = row_max + jnp.log(row_total)
    chances = jnp.exp(scores - log_norm).astype(jnp.bfloat16)
    context = jnp.einsum("shqk,skhe->sqhe", chances, value_rows, preferred_element_type=jnp.float32)
    return (context, log_norm)


def attend_back(queries, key_rows, value_rows, log_norm, context_grad):
    chances = jnp.exp(scores_of(queries, key_rows) - log_norm)
    chance_grad = jnp.einsum(
        "sqhe,skhe->shqk", context_grad, value_rows, preferred_element_type=jnp.float32
    )
    value_grad = jnp.einsum(
        "shqk,sqhe->skhe",
        chances.astype(jnp.bfloat16),
        context_grad,
        preferred_element_type=jnp.float32,
    )
    inner = jnp.sum(chance_grad * chances, axis=-1, keepdims=True)
    score_grad = (chances * (chance_grad - inner)).astype(jnp.bfloat16)
    query_grad = jnp.einsum(
        "shqk,skhe->sqhe", score_grad, key_rows, preferred_element_type=jnp.float32
    ) * HEAD_DIM ** (-0.5)
    key_grad = jnp.einsum(
        "shqk,sqhe->skhe", score_grad, queries, preferred_element_type=jnp.float32
    ) * HEAD_DIM ** (-0.5)
    return (query_grad, key_grad, value_grad)


def layer_forward(hidden, weights, whole, layer_index, slot_count):
    (
        attn_gain,
        attn_shift,
        qkv_weight,
        qv_bias,
        proj_weight,
        proj_bias,
        mlp_gain,
        mlp_shift,
        up_weight,
        up_bias,
        down_weight,
        down_bias,
    ) = weights
    local_width = qkv_weight.shape[2]
    qkv_flat = whole[0][layer_index]
    normed = layer_norm(hidden, attn_gain, attn_shift).astype(jnp.bfloat16)
    joined = jnp.dot(normed, qkv_flat, preferred_element_type=jnp.float32).reshape(
        -1, 3, local_width
    )
    queries = (joined[:, 0] + qv_bias[0]).astype(jnp.bfloat16)
    key_rows = joined[:, 1].astype(jnp.bfloat16)
    value_rows = (joined[:, 2] + qv_bias[1]).astype(jnp.bfloat16)
    context, log_norm = attend(
        split_heads(queries, slot_count),
        split_heads(key_rows, slot_count),
        split_heads(value_rows, slot_count),
    )
    context = context.reshape(-1, local_width).astype(jnp.bfloat16)
    attn_total = product_sum(context, whole[1], layer_index, False, 4 * layer_index)
    residual = hidden + attn_total.astype(jnp.float32) + proj_bias
    mlp_input = layer_norm(residual, mlp_gain, mlp_shift).astype(jnp.bfloat16)
    pre_act = jnp.dot(mlp_input, up_weight, preferred_element_type=jnp.float32) + up_bias
    activ = gelu_exact(pre_act).astype(jnp.bfloat16)
    mlp_total = product_sum(activ, whole[3], layer_index, False, 4 * layer_index + 1)
    output = residual + mlp_total.astype(jnp.float32) + down_bias
    saved = (
        hidden,
        normed,
        queries,
        key_rows,
        value_rows,
        log_norm,
        context,
        residual,
        mlp_input,
        pre_act,
        activ,
    )
    return (output, saved)


def layer_backward(out_grad, weights, whole, layer_index, saved, slot_count):
    (
        attn_gain,
        attn_shift,
        qkv_weight,
        qv_bias,
        proj_weight,
        proj_bias,
        mlp_gain,
        mlp_shift,
        up_weight,
        up_bias,
        down_weight,
        down_bias,
    ) = weights
    (
        hidden,
        normed,
        queries,
        key_rows,
        value_rows,
        log_norm,
        context,
        residual,
        mlp_input,
        pre_act,
        activ,
    ) = saved
    local_width = qkv_weight.shape[2]
    down_bias_grad = row_sum(out_grad)
    branch_grad = out_grad.astype(jnp.bfloat16)
    down_weight_grad = weight_grad_start(branch_grad, activ)
    activ_grad = jnp.einsum(
        "rd,fd->rf", branch_grad, down_weight, preferred_element_type=jnp.float32
    )
    gelu_pull = jax.vjp(gelu_exact, pre_act)[1]
    pre_grad = gelu_pull(activ_grad)[0].astype(jnp.bfloat16)
    up_bias_grad = row_sum(pre_grad)
    up_weight_grad = weight_grad_start(mlp_input, pre_grad)
    pre_grad = after(pre_grad, down_weight_grad, up_weight_grad)
    mlp_input_grad = product_sum(pre_grad, whole[2], layer_index, True, 4 * layer_index + 2)
    mlp_input_grad = mlp_input_grad.astype(jnp.float32)
    mlp_pull = jax.vjp(
        layer_norm, residual, mlp_gain.astype(jnp.float32), mlp_shift.astype(jnp.float32)
    )[1]
    resid_part, mlp_gain_grad, mlp_shift_grad = mlp_pull(mlp_input_grad)
    residual_grad = out_grad + resid_part
    proj_bias_grad = row_sum(residual_grad)
    attn_branch = residual_grad.astype(jnp.bfloat16)
    proj_weight_grad = weight_grad_start(attn_branch, context)
    context_grad = jnp.einsum(
        "rd,cd->rc", attn_branch, proj_weight, preferred_element_type=jnp.float32
    ).astype(jnp.bfloat16)
    query_grad, key_grad, value_grad = attend_back(
        split_heads(queries, slot_count),
        split_heads(key_rows, slot_count),
        split_heads(value_rows, slot_count),
        log_norm,
        split_heads(context_grad, slot_count),
    )
    query_grad = query_grad.reshape(-1, local_width).astype(jnp.bfloat16)
    key_grad = key_grad.reshape(-1, local_width).astype(jnp.bfloat16)
    value_grad = value_grad.reshape(-1, local_width).astype(jnp.bfloat16)
    qv_bias_grad = jnp.stack([row_sum(query_grad), row_sum(value_grad)])
    flat_grad = jnp.stack([query_grad, key_grad, value_grad], axis=1).reshape(-1, 3 * local_width)
    qkv_weight_grad = weight_grad_start(normed, flat_grad)
    flat_grad = after(flat_grad, proj_weight_grad, qkv_weight_grad)
    normed_grad = product_sum(flat_grad, whole[0], layer_index, True, 4 * layer_index + 3)
    normed_grad = normed_grad.astype(jnp.float32)
    attn_pull = jax.vjp(
        layer_norm, hidden, attn_gain.astype(jnp.float32), attn_shift.astype(jnp.float32)
    )[1]
    hidden_part, attn_gain_grad, attn_shift_grad = attn_pull(normed_grad)
    grads = (
        attn_gain_grad,
        attn_shift_grad,
        qkv_weight_grad,
        qv_bias_grad,
        proj_weight_grad,
        proj_bias_grad,
        mlp_gain_grad,
        mlp_shift_grad,
        up_weight_grad,
        up_bias_grad,
        down_weight_grad,
        down_bias_grad,
    )
    return (residual_grad + hidden_part, grads)


def halve_exchange(blocks, bit):
    members = lax.axis_size("dp")
    mine = lax.rem(lax.div(lax.axis_index("dp"), bit), 2)
    perm = [(member, member ^ bit) for member in range(members)]
    away = lax.dynamic_index_in_dim(blocks, 1 - mine, 1, keepdims=False)
    kept = lax.dynamic_index_in_dim(blocks, mine, 1, keepdims=False)
    got = lax.ppermute(away.astype(jnp.bfloat16), "dp", perm)
    return kept.astype(jnp.float32) + got.astype(jnp.float32)


def scatter_rest(blocks, bit):
    members = lax.axis_size("dp")
    while bit < members:
        blocks = blocks.reshape((blocks.shape[0] // 2, 2) + blocks.shape[1:])
        blocks = halve_exchange(blocks, bit)
        bit *= 2
    return blocks[0]


def weight_grad_start(left, right):
    members = lax.axis_size("dp")
    rows = left.shape[0]
    mine = lax.rem(lax.axis_index("dp"), 2)
    split = left.reshape(rows, members // 2, 2, -1)
    width = split.shape[3]
    halves = []
    for index in (1 - mine, mine):
        half = lax.dynamic_index_in_dim(split, index, 2, keepdims=False).reshape(rows, -1)
        halves.append(
            jnp.einsum("rd,rf->df", half, right, preferred_element_type=jnp.float32).astype(
                jnp.bfloat16
            )
        )
    perm = [(member, member ^ 1) for member in range(members)]
    got = lax.ppermute(halves[0], "dp", perm)
    return (halves[1], got, width)


def after(value, *started):
    return lax.optimization_barrier((value,) + tuple(pair[0] for pair in started))[0]


def weight_grad_end(started):
    kept, got, width = started
    total = kept.astype(jnp.float32) + got.astype(jnp.float32)
    return scatter_rest(total.reshape(-1, width, total.shape[1]), 2)


def sum_vectors(vectors):
    members = lax.axis_size("dp")
    rows = [vector.reshape(members, -1) for vector in vectors]
    sizes = [row.shape[1] for row in rows]
    line = jnp.concatenate(rows, axis=1)[:, None, :]
    line = scatter_rest(line, 1)[0]
    parts = []
    at = 0
    for size in sizes:
        parts.append(line[at : at + size])
        at += size
    return parts


def sum_layer(grads):
    (
        attn_gain_grad,
        attn_shift_grad,
        qkv_started,
        qv_bias_grad,
        proj_started,
        proj_bias_grad,
        mlp_gain_grad,
        mlp_shift_grad,
        up_started,
        up_bias_grad,
        down_started,
        down_bias_grad,
    ) = grads
    vectors = sum_vectors(
        [
            attn_gain_grad,
            attn_shift_grad,
            proj_bias_grad,
            mlp_gain_grad,
            mlp_shift_grad,
            down_bias_grad,
            up_bias_grad,
            qv_bias_grad[0],
            qv_bias_grad[1],
        ]
    )
    down_part = weight_grad_end(down_started)
    up_part = weight_grad_end(up_started)
    proj_part = weight_grad_end(proj_started)
    qkv_part = weight_grad_end(qkv_started)
    return (
        vectors[0],
        vectors[1],
        qkv_part.reshape(qkv_part.shape[0], 3, -1),
        jnp.stack([vectors[7], vectors[8]]),
        proj_part.T,
        vectors[2],
        vectors[3],
        vectors[4],
        up_part,
        vectors[6],
        down_part.T,
        vectors[5],
    )


def on_device(
    images,
    upstream,
    placed,
    attn_gain,
    attn_shift,
    qkv_weight,
    qv_bias,
    proj_weight,
    proj_bias,
    mlp_gain,
    mlp_shift,
    up_weight,
    up_bias,
    down_weight,
    down_bias,
):
    slot_count = images.shape[0]
    row_count = slot_count * images.shape[1]
    model_width = images.shape[2]
    retain_mask = placed.astype(jnp.float32)[:, None, None]
    params = (
        attn_gain,
        attn_shift,
        qkv_weight,
        qv_bias,
        proj_weight,
        proj_bias,
        mlp_gain,
        mlp_shift,
        up_weight,
        up_bias,
        down_weight,
        down_bias,
    )
    qkv_whole = qkv_weight.reshape(qkv_weight.shape[0], qkv_weight.shape[1], -1)
    whole = (qkv_whole, proj_weight, up_weight, down_weight)
    hidden = images.reshape(row_count, model_width).astype(jnp.float32)
    saved_layers = []
    for layer_index in range(LAYERS):
        weights = tuple((param[layer_index] for param in params))
        hidden, saved = layer_forward(hidden, weights, whole, layer_index, slot_count)
        saved_layers.append(saved)
    outputs = (hidden.reshape(images.shape) * retain_mask).astype(jnp.bfloat16)
    carried = (upstream.astype(jnp.float32) * retain_mask).reshape(row_count, model_width)
    collected = [None] * LAYERS
    for layer_index in reversed(range(LAYERS)):
        weights = tuple((param[layer_index] for param in params))
        carried, layer_grads = layer_backward(
            carried, weights, whole, layer_index, saved_layers[layer_index], slot_count
        )
        collected[layer_index] = sum_layer(layer_grads)
    stacked = tuple(
        (
            jnp.stack([collected[layer_index][member] for layer_index in range(LAYERS)])
            for member in range(12)
        )
    )
    images_grad = carried.reshape(images.shape).astype(jnp.bfloat16)
    return (
        outputs,
        images_grad,
        stacked[0],
        stacked[1],
        stacked[2],
        stacked[3],
        stacked[4],
        stacked[5],
        stacked[6],
        stacked[7],
        stacked[8],
        stacked[9],
        stacked[10],
        stacked[11],
    )


def solution(mesh):
    return jax.shard_map(
        on_device,
        mesh=mesh,
        in_specs=(
            P("dp", None, None),
            P("dp", None, None),
            P("dp"),
            P(),
            P(),
            P(None, None, None, "tensor"),
            P(None, None, "tensor"),
            P(None, "tensor", None),
            P(),
            P(),
            P(),
            P(None, None, "tensor"),
            P(None, "tensor"),
            P(None, "tensor", None),
            P(),
        ),
        out_specs=(
            P("dp", None, None),
            P("dp", None, None),
            P(None, "dp"),
            P(None, "dp"),
            P(None, "dp", None, "tensor"),
            P(None, None, ("tensor", "dp")),
            P(None, "tensor", "dp"),
            P(None, "dp"),
            P(None, "dp"),
            P(None, "dp"),
            P(None, "dp", "tensor"),
            P(None, ("tensor", "dp")),
            P(None, "tensor", "dp"),
            P(None, "dp"),
        ),
        check_vma=False,
    )
```
